32 devices in a mesh: rep: 4 (over y, core), fsdp: 8 (over z, x).
Axes of the slice: x: 2, y: 2, z: 4, core: 2. Of those that a mesh axis runs over, the one named last changes fastest.
Arguments:
- clip_tokens: bfloat16 [4096, 6144], P(('rep', 'fsdp')), may hold values from -6 to 6
- frame_ids: int32 [4096], P(('rep', 'fsdp')), may hold values from 0 to 15
- modulation: float32 [16, 6144], replicated, may hold values from -3 to 3
- query_gain: float32 [128], replicated, may hold values from 0.1 to 1.9
- query_weight: bfloat16 [4, 6144, 3072], P('rep', 'fsdp'), may hold values from -0.078125 to 0.078125
- query_cotangent: bfloat16 [4096, 3072], P(('rep', 'fsdp')), may hold values from -6 to 6
- pseudo_grad: float32 [4, 524288], P('rep', 'fsdp'), may hold values from -6 to 6
- outer_params: float32 [524288], P('fsdp'), may hold values from -6 to 6
- outer_momentum: float32 [524288], P('fsdp'), may hold values from -3 to 3
Outputs:
- input_grad: bfloat16 [4096, 6144], P(('rep', 'fsdp'))
- weight_grad: bfloat16 [4, 6144, 3072], P('rep', 'fsdp')
- table_grad: float32 [4, 16, 6144], P('rep', None, 'fsdp')
- new_fragment: float32 [524288], P('fsdp')
- new_momentum: float32 [524288], P('fsdp')
The draws below stay inside these ranges and needn't reach their ends.
All inputs are finite; a program needn't handle non-finite values.
Results may differ from the reference program's by a relative error of at most 0.02.
Values may be sent and summed in bfloat16 or wider, within the bound.
A program may use at most 128 MiB of HBM per device.

```python
import jax
import jax.numpy as jnp
from jax import lax

D = 6144
HEAD = 128
E = 3072
FRAMES = 16
TOK_DEV = 128
ROWS = 4096
FRAG = 524288
N_REP = 4
N_FSDP = 8


def touch_ends(drawn, stream_key, least, largest):
    index_at = [jax.random.randint(jax.random.fold_in(stream_key, axis), (), 0, length) for axis, length in enumerate(drawn.shape)]
    widest = drawn.shape.index(max(drawn.shape))
    neighbour = index_at[:widest] + [(index_at[widest] + 1) % drawn.shape[widest]] + index_at[widest + 1:]
    return drawn.at[tuple(index_at)].set(least).at[tuple(neighbour)].set(largest)


def block_levels(own_key, extent, pieces, smallest, high):
    gain = 1.0
    for position, parts in pieces:
        heights = jax.random.uniform(jax.random.fold_in(jax.random.fold_in(own_key, 6), position), (parts,), jnp.float32, smallest / len(pieces), high / len(pieces))
        gain = gain * jnp.repeat(jnp.exp(heights), extent[position] // parts).reshape((-1,) + (1,) * (len(extent) - 1 - position))
    return gain


def centred(stream_key, shape, deviation, bound, pieces=(), held_as=jnp.bfloat16):
    gain = block_levels(stream_key, shape, pieces, -0.22, 0.18) if pieces else 1.0
    drawn = jax.random.normal(stream_key, shape, jnp.float32) * deviation * gain
    return jnp.minimum(jnp.maximum(drawn, -bound), bound).astype(held_as)


def setup_inputs(seed: int = 0) -> dict:
    key_list = jax.random.split(jax.random.key(seed), 10)
    return {
        "clip_tokens": centred(key_list[0], (ROWS, D), 1.0, 6.0, ((0, 32),)),
        "frame_ids": touch_ends(jax.random.randint(key_list[1], (ROWS,), 0, FRAMES), jax.random.fold_in(key_list[1], 1), 0, FRAMES - 1).astype(jnp.int32),
        "modulation": centred(key_list[2], (FRAMES, D), 0.5, 3.0, (), jnp.float32),
        "query_gain": jnp.clip(1.0 + 0.18 * jax.random.normal(key_list[3], (HEAD,), jnp.float32), 0.1, 1.9),
        "query_weight": centred(key_list[4], (N_REP, D, E), D ** -0.5, 0.078125, ((0, 4), (1, 8))),
        "query_cotangent": centred(key_list[5], (ROWS, E), 1.0, 6.0, ((0, 32),)),
        "pseudo_grad": centred(key_list[6], (N_REP, FRAG), 1.0, 6.0, ((0, 4), (1, 8)), jnp.float32),
        "outer_params": centred(key_list[7], (FRAG,), 1.0, 6.0, ((0, 8),), jnp.float32),
        "outer_momentum": centred(key_list[8], (FRAG,), 0.5, 3.0, ((0, 8),), jnp.float32),
    }


EPSILON = 1e-06
OUTER_RATE = 0.7
OUTER_MOMENTUM = 0.9

def replica_backward(operands):
    tokens, frames, modulation, query_gain, weight, cotangent = operands
    rows_all = tokens.shape[0]
    tokens_f = tokens.astype(jnp.float32)
    inverse = lax.rsqrt(lax.optimization_barrier(jnp.mean(tokens_f * tokens_f, axis=-1, keepdims=True)) + EPSILON)
    normed = tokens_f * inverse
    frame_mod = modulation[frames]
    normal_in = (normed * (1.0 + frame_mod)).astype(jnp.bfloat16)
    width_part = D // N_FSDP
    blocks = normal_in.reshape(rows_all, N_FSDP, width_part).transpose(1, 0, 2)
    weight_blocks = weight.reshape(N_FSDP, width_part, E)

    def add_block(total, pair):
        partial_sum = jnp.dot(pair[0], pair[1], preferred_element_type=jnp.float32).astype(jnp.bfloat16)
        partial_sum = lax.optimization_barrier(partial_sum)
        return (total + partial_sum.astype(jnp.float32), None)
    projected, unused = lax.scan(add_block, jnp.zeros((rows_all, E), jnp.float32), (blocks, weight_blocks))
    heads = projected.reshape(rows_all, E // HEAD, HEAD)
    head_inv = lax.rsqrt(lax.optimization_barrier(jnp.mean(heads * heads, axis=-1, keepdims=True)) + EPSILON)
    head_hat = heads * head_inv
    scaled = cotangent.astype(jnp.float32).reshape(rows_all, E // HEAD, HEAD) * query_gain
    head_grad = head_inv * (scaled - head_hat * lax.optimization_barrier(jnp.mean(scaled * head_hat, axis=-1, keepdims=True)))
    proj_grad = head_grad.reshape(rows_all, E).astype(jnp.bfloat16)
    weight_grad = lax.dot_general(normal_in, proj_grad, (((0,), (0,)), ((), ())), preferred_element_type=jnp.float32).astype(jnp.bfloat16)
    normal_grad = lax.dot_general(proj_grad, weight, (((1,), (1,)), ((), ())), preferred_element_type=jnp.float32).astype(jnp.bfloat16)
    normal_grad = lax.optimization_barrier(normal_grad).astype(jnp.float32)
    table_grad = jax.ops.segment_sum(normal_grad * normed, frames, num_segments=FRAMES)
    grad_hat = normal_grad * (1.0 + frame_mod)
    input_grad = inverse * (grad_hat - normed * lax.optimization_barrier(jnp.mean(grad_hat * normed, axis=-1, keepdims=True)))
    return (input_grad.astype(jnp.bfloat16), weight_grad, table_grad)

def reference(clip_tokens, frame_ids, modulation, query_gain, query_weight, query_cotangent, pseudo_grad, outer_params, outer_momentum):
    group_rows = TOK_DEV * N_FSDP
    token_groups = clip_tokens.reshape(N_REP, group_rows, D)
    frame_groups = frame_ids.reshape(N_REP, group_rows)
    grad_groups = query_cotangent.reshape(N_REP, group_rows, E)

    def one_replica(operands):
        return replica_backward((operands[0], operands[1], modulation, query_gain, operands[2], operands[3]))
    input_grad, weight_grad, table_grad = lax.map(one_replica, (token_groups, frame_groups, query_weight, grad_groups))
    average = lax.optimization_barrier(jnp.sum(pseudo_grad, axis=0)) / N_REP
    new_momentum = OUTER_MOMENTUM * outer_momentum + average
    new_fragment = outer_params - OUTER_RATE * (average + OUTER_MOMENTUM * new_momentum)
    return (input_grad.reshape(ROWS, D), weight_grad, table_grad, new_fragment, new_momentum)
```

```python
import jax
import jax.numpy as jnp
from jax import lax
from jax.sharding import PartitionSpec as P

EPSILON = 1e-06
OUTER_RATE = 0.7
OUTER_MOMENTUM = 0.9
CHUNKS = 4


def shards(
    clip_tokens,
    frame_ids,
    modulation,
    query_gain,
    query_weight,
    query_cotangent,
    pseudo_grad,
    outer_params,
    outer_momentum,
):
    n = lax.axis_size("fsdp")
    me = lax.axis_index("fsdp")
    rows, width = clip_tokens.shape
    part = width // n
    weight_rows = query_weight[0]
    columns = weight_rows.shape[1]
    head_size = query_gain.shape[0]
    frame_count = modulation.shape[0]
    f32 = jnp.float32

    def swap(value, k):
        return lax.ppermute(value, "fsdp", [(i, i ^ k) for i in range(n)])

    def column_block(value, k):
        return lax.dynamic_slice_in_dim(value, (me ^ k) * part, part, 1)

    tokens_all = jnp.concatenate(
        [column_block(clip_tokens, 0)] + [swap(column_block(clip_tokens, k), k) for k in range(1, n)], 0
    )
    tokens_f = clip_tokens.astype(f32)
    inverse = lax.rsqrt(jnp.mean(tokens_f * tokens_f, axis=-1, keepdims=True) + EPSILON)
    sides = jnp.stack([inverse[:, 0], frame_ids.astype(f32)])
    sides_all = lax.all_gather(sides, "fsdp", axis=0)
    sides_all = jnp.stack([lax.dynamic_index_in_dim(sides_all, me ^ k, 0, False) for k in range(n)])
    inverse_all = sides_all[:, 0].reshape(n * rows, 1)
    frames_all = sides_all[:, 1].reshape(n * rows, 1)
    one_hot_all = (frames_all == jnp.arange(frame_count, dtype=f32)[None, :]).astype(f32)
    normed_all = tokens_all.astype(f32) * inverse_all
    mod_all = jnp.dot(one_hot_all, column_block(modulation, 0), precision=lax.Precision.HIGHEST)
    normal_in = (normed_all * (1.0 + mod_all)).astype(jnp.bfloat16)

    chunk = columns // CHUNKS
    weight_parts = []
    feature_total = jnp.zeros((n * rows, part), f32)
    for c in range(CHUNKS):
        weight_c = weight_rows[:, c * chunk : (c + 1) * chunk]
        partial = jnp.dot(normal_in, weight_c, preferred_element_type=f32).astype(jnp.bfloat16)
        partial = partial.reshape(n // 2, 2, rows, chunk)
        pair = partial[:, 0].astype(f32) + swap(partial[:, 1], 1).astype(f32)
        pair_sent = pair.astype(jnp.bfloat16)
        projected = pair[0]
        for k in range(1, n // 2):
            projected = projected + swap(pair_sent[k], 2 * k).astype(f32)
        heads = projected.reshape(rows, chunk // head_size, head_size)
        head_inv = lax.rsqrt(jnp.mean(heads * heads, axis=-1, keepdims=True) + EPSILON)
        head_hat = heads * head_inv
        cotangent = query_cotangent[:, c * chunk : (c + 1) * chunk].astype(f32)
        scaled = cotangent.reshape(heads.shape) * query_gain
        head_grad = head_inv * (
            scaled - head_hat * jnp.mean(scaled * head_hat, axis=-1, keepdims=True)
        )
        proj_grad = head_grad.reshape(rows, chunk).astype(jnp.bfloat16)
        line = jnp.stack([proj_grad] + [swap(proj_grad, 2 * k) for k in range(1, n // 2)])
        piece = jnp.stack([line, swap(line, 1)], axis=1).reshape(n * rows, chunk)
        weight_parts.append(
            lax.dot_general(
                normal_in, piece, (((0,), (0,)), ((), ())), preferred_element_type=f32
            ).astype(jnp.bfloat16)
        )
        feature_total = feature_total + lax.dot_general(
            piece, weight_c, (((1,), (1,)), ((), ())), preferred_element_type=f32
        )
    weight_grad = jnp.concatenate(weight_parts, axis=1)[None]
    feature = feature_total.astype(jnp.bfloat16)
    table_grad = lax.dot_general(
        one_hot_all,
        feature.astype(f32) * normed_all,
        (((0,), (0,)), ((), ())),
        precision=lax.Precision.HIGHEST,
    )[None]

    blocks = feature.reshape(n, rows, part)
    normal_grad = jnp.zeros((rows, width), jnp.bfloat16)
    for k in range(n):
        arrived = blocks[0] if k == 0 else swap(blocks[k], k)
        normal_grad = lax.dynamic_update_slice_in_dim(normal_grad, arrived, (me ^ k) * part, 1)
    normal_grad = normal_grad.astype(f32)
    normed = tokens_f * inverse
    one_hot = (frame_ids[:, None] == jnp.arange(frame_count, dtype=jnp.int32)[None, :]).astype(f32)
    frame_mod = jnp.dot(one_hot, modulation, precision=lax.Precision.HIGHEST)
    grad_hat = normal_grad * (1.0 + frame_mod)
    input_grad = (
        inverse * (grad_hat - normed * jnp.mean(grad_hat * normed, axis=-1, keepdims=True))
    ).astype(jnp.bfloat16)
    replicas = lax.axis_size("rep")
    average = lax.psum(pseudo_grad[0].astype(jnp.bfloat16), "rep").astype(f32) / replicas
    new_momentum = OUTER_MOMENTUM * outer_momentum + average
    new_fragment = outer_params - OUTER_RATE * (average + OUTER_MOMENTUM * new_momentum)
    return (input_grad, weight_grad, table_grad, new_fragment, new_momentum)


def solution(mesh):
    placed = (
        P(("rep", "fsdp"), None),
        P(("rep", "fsdp")),
        P(),
        P(),
        P("rep", "fsdp", None),
        P(("rep", "fsdp"), None),
        P("rep", "fsdp"),
        P("fsdp"),
        P("fsdp"),
    )
    return jax.shard_map(
        shards,
        mesh=mesh,
        in_specs=placed,
        out_specs=(
            P(("rep", "fsdp"), None),
            P("rep", "fsdp", None),
            P("rep", None, "fsdp"),
            P("fsdp"),
            P("fsdp"),
        ),
        check_vma=False,
    )
```

```python
import functools

import jax
import jax.numpy as jnp
from jax import lax
from jax.experimental import pallas as pl
from jax.experimental.pallas import tpu as pltpu
from jax.sharding import PartitionSpec as P

EPSILON = 1e-06
OUTER_RATE = 0.7
OUTER_MOMENTUM = 0.9
CHUNKS = 4
TILE = 256
MESH = pl.DeviceIdType.MESH
EXACT = lax.Precision.HIGHEST
f32 = jnp.float32
bf16 = jnp.bfloat16


def partner(index, offset):
    bit = 1
    moved = index
    while bit <= offset:
        if offset & bit:
            moved = moved + bit * (1 - 2 * ((index // bit) % 2))
        bit *= 2
    return moved


def kernel(
    n,
    replicas,
    x_ref,
    frames_ref,
    mod_ref,
    gain_ref,
    w_hbm,
    cot_hbm,
    pseudo_ref,
    params_ref,
    momentum_ref,
    grad_ref,
    dw_hbm,
    table_ref,
    fragment_out,
    momentum_out,
    w_vmem,
    cot_vmem,
    sides,
    x_all,
    ni,
    ni_t,
    p_send,
    p_keep,
    p_pair,
    p_line,
    p_own,
    gathered,
    dw_vmem,
    dx_sum,
    dx_recv,
    outer_send,
    outer_recv,
    local_sem,
    dw_sem,
    outer_sem,
    x_sem,
    side_sem,
    pair_sem,
    line_sem,
    gather_line_sem,
    gather_pair_sem,
    dx_sem,
):
    dx_send = ni
    me = lax.axis_index("fsdp")
    rep = lax.axis_index("rep")
    half = n // 2
    rows = x_ref.shape[0]
    part = x_ref.shape[1] // n
    chunk = w_vmem.shape[1] // CHUNKS
    head = gain_ref.shape[1]
    frame_count = mod_ref.shape[0]
    at = [partner(me, k) for k in range(n)]
    slot = [(k % 2) * half + k // 2 for k in range(n)]

    def send(src, dst, sems, where, k):
        return pltpu.make_async_remote_copy(
            src_ref=src,
            dst_ref=dst,
            send_sem=sems.at[(0, *where)],
            recv_sem=sems.at[(1, *where)],
            device_id={"fsdp": at[k]},
            device_id_type=MESH,
        )

    def columns(k):
        return pl.ds(pl.multiple_of(at[k] * part, 128), part)

    load_w = pltpu.make_async_copy(w_hbm, w_vmem, local_sem.at[0])
    load_cot = pltpu.make_async_copy(cot_hbm, cot_vmem, local_sem.at[1])
    load_w.start()
    load_cot.start()
    outer_send[...] = pseudo_ref[...].astype(bf16)

    barrier = pltpu.get_barrier_semaphore()
    for k in range(1, n):
        pl.semaphore_signal(barrier, inc=1, device_id={"fsdp": at[k]}, device_id_type=MESH)
    for k in range(1, replicas):
        pl.semaphore_signal(
            barrier, inc=1, device_id={"rep": partner(rep, k)}, device_id_type=MESH
        )
    pl.semaphore_wait(barrier, n + replicas - 2)

    order = sorted(range(1, n), key=lambda k: -k)
    x_copies = {}
    for k in order:
        x_copies[k] = send(x_ref.at[:, columns(k)], x_all.at[slot[k]], x_sem, (k,), k)
        x_copies[k].start()

    x_f = x_ref[...].astype(f32)
    inverse = lax.rsqrt(jnp.mean(x_f * x_f, axis=-1, keepdims=True) + EPSILON)
    lane = lax.broadcasted_iota(jnp.int32, (rows, rows), 1)
    row = lax.broadcasted_iota(jnp.int32, (rows, rows), 0)
    eye = (lane == row).astype(f32)
    contract_last = (((1,), (1,)), ((), ()))
    inverse_row = jnp.sum(eye * inverse, axis=0, keepdims=True)
    side_row = lax.broadcasted_iota(jnp.int32, (8, rows), 0)
    sides[0] = jnp.where(side_row == 0, inverse_row, frames_ref[...].astype(f32))
    side_copies = {}
    for k in order:
        side_copies[k] = send(sides.at[0], sides.at[slot[k]], side_sem, (k,), k)
        side_copies[k].start()

    outer_copies = []
    for k in range(1, replicas):
        copy = pltpu.make_async_remote_copy(
            src_ref=outer_send,
            dst_ref=outer_recv.at[k - 1],
            send_sem=outer_sem.at[0, k - 1],
            recv_sem=outer_sem.at[1, k - 1],
            device_id={"rep": partner(rep, k)},
            device_id_type=MESH,
        )
        copy.start()
        outer_copies.append(copy)

    def as_columns(s):
        return lax.dot_general(
            eye, sides[s], contract_last, precision=EXACT, preferred_element_type=f32
        )

    frame_lane = lax.broadcasted_iota(jnp.int32, (rows, frame_count), 1).astype(f32)

    def modulated(cols, block):
        one_hot = (cols[:, 1:2] == frame_lane).astype(f32)
        return 1.0 + jnp.dot(one_hot, block, precision=EXACT, preferred_element_type=f32)

    own_columns = as_columns(0)
    own_mod = mod_ref[:, columns(0)]
    x_all[0] = x_ref[:, columns(0)]
    for k in [0] + order[::-1]:
        s = slot[k]
        if k:
            x_copies[k].wait_recv()
            side_copies[k].wait_recv()
        cols = as_columns(s)
        value = x_all[s].astype(f32) * cols[:, 0:1] * modulated(cols, own_mod)
        ni[s] = value.astype(bf16)
        ni_t[:, s * rows : (s + 1) * rows] = value.T.astype(bf16)
    load_w.wait()
    load_cot.wait()

    def tiles(total, body):
        size = TILE if total % TILE == 0 else TILE // 2
        lax.fori_loop(0, total // size, lambda j, carry: (body(j, size), carry)[1], 0)

    pair_copies = []
    for c in range(CHUNKS):
        for kx, target in ((1, p_send), (0, p_keep)):
            left = ni[kx * half : (kx + 1) * half].reshape(half * rows, part)

            def project(j, size, c=c, left=left, target=target):
                w = w_vmem[:, pl.ds(pl.multiple_of(c * chunk + j * size, size), size)]
                value = jnp.dot(left, w, preferred_element_type=f32).astype(bf16)
                target[c, :, :, pl.ds(pl.multiple_of(j * size, size), size)] = value.reshape(
                    half, rows, size
                )

            tiles(chunk, project)
            if kx == 1:
                copy = send(p_send.at[c], p_pair.at[c], pair_sem, (c,), 1)
                copy.start()
                pair_copies.append(copy)

    line_copies, gather_line, gather_pair = {}, {}, {}

    def reduce_pair(c):
        pair_copies[c].wait_recv()
        for kz in list(range(1, half))[::-1]:
            p_keep[c, kz] = (p_keep[c, kz].astype(f32) + p_pair[c, kz].astype(f32)).astype(bf16)
            line_copies[c, kz] = send(
                p_keep.at[c, kz], p_line.at[c, kz - 1], line_sem, (c, kz), 2 * kz
            )
            line_copies[c, kz].start()
        p_own[c % 2] = p_keep[c, 0].astype(f32) + p_pair[c, 0].astype(f32)

    def head_grads(c):
        for kz in range(1, half):
            line_copies[c, kz].wait_recv()
        gain = gain_ref[...]
        for h in range(chunk // head):
            span = slice(h * head, (h + 1) * head)
            projected = p_own[c % 2, :, span]
            for kz in range(1, half):
                projected = projected + p_line[c, kz - 1, :, span].astype(f32)
            head_inv = lax.rsqrt(
                jnp.mean(projected * projected, axis=-1, keepdims=True) + EPSILON
            )
            head_hat = projected * head_inv
            scaled = cot_vmem[:, c * chunk + h * head : c * chunk + (h + 1) * head].astype(f32) * gain
            mean = jnp.mean(scaled * head_hat, axis=-1, keepdims=True)
            gathered[c, 0, 0, :, span] = (head_inv * (scaled - head_hat * mean)).astype(bf16)
        for kz in list(range(1, half))[::-1]:
            gather_line[c, kz] = send(
                gathered.at[c, 0, 0], gathered.at[c, 0, kz], gather_line_sem, (c, kz), 2 * kz
            )
            gather_line[c, kz].start()
        gather_pair[c, 0] = send(
            gathered.at[c, 0, 0], gathered.at[c, 1, 0], gather_pair_sem, (c, 0), 1
        )
        gather_pair[c, 0].start()

    def forward(c):
        for kz in range(1, half):
            gather_line[c, kz].wait_recv()
            gather_pair[c, kz] = send(
                gathered.at[c, 0, kz], gathered.at[c, 1, kz], gather_pair_sem, (c, kz), 1
            )
            gather_pair[c, kz].start()

    def feature(c):
        for kz in range(half):
            gather_pair[c, kz].wait_recv()
        g = gathered[c].reshape(n * rows, chunk)

        def body(j, size):
            span = pl.ds(pl.multiple_of(j * size, size), size)
            w = w_vmem[span, c * chunk : (c + 1) * chunk]
            value = lax.dot_general(g, w, contract_last, preferred_element_type=f32)
            if c > 0:
                value = value + dx_sum[:, span]
            if c < CHUNKS - 1:
                dx_sum[:, span] = value
            else:
                dx_send[:, :, span] = value.astype(bf16).reshape(n, rows, size)

        tiles(part, body)

    dw_copies = []

    def weight(c):
        if c >= 2:
            dw_copies[c - 2].wait()
        g = gathered[c].reshape(n * rows, chunk)

        def body(j, size):
            span = pl.ds(pl.multiple_of(j * size, size), size)
            dw_vmem[c % 2, span, :] = jnp.dot(
                ni_t[span, :], g, preferred_element_type=f32
            ).astype(bf16)

        tiles(part, body)
        span = slice(c * chunk, (c + 1) * chunk)
        copy = pltpu.make_async_copy(dw_vmem.at[c % 2], dw_hbm.at[:, span], dw_sem.at[c])
        copy.start()
        dw_copies.append(copy)

    for t in range(CHUNKS + 3):
        if t < CHUNKS:
            reduce_pair(t)
        if 0 <= t - 1 < CHUNKS:
            head_grads(t - 1)
        if 0 <= t - 2 < CHUNKS:
            forward(t - 2)
        if 0 <= t - 3 < CHUNKS:
            feature(t - 3)
            if t - 3 < CHUNKS - 1:
                weight(t - 3)

    dx_copies = {}
    for k in order:
        dx_copies[k] = send(dx_send.at[slot[k]], dx_recv.at[slot[k]], dx_sem, (k,), k)
        dx_copies[k].start()
    weight(CHUNKS - 1)

    frame_row = lax.broadcasted_iota(jnp.int32, (frame_count, rows), 0).astype(f32)
    table = jnp.zeros((frame_count, part), f32)
    for s in range(n):
        normed = x_all[s].astype(f32) * as_columns(s)[:, 0:1]
        picked = (sides[s, 1:2, :] == frame_row).astype(f32)
        table = table + jnp.dot(
            picked, dx_send[s].astype(f32) * normed, precision=EXACT, preferred_element_type=f32
        )
    table_ref[...] = table

    for copy in outer_copies:
        copy.wait_recv()
    terms = [outer_send[...].astype(f32)] + [
        outer_recv[k - 1].astype(f32) for k in range(1, replicas)
    ]
    while len(terms) > 1:
        terms = [terms[i] + terms[i + 1] for i in range(0, len(terms), 2)]
    average = terms[0] / replicas
    new_momentum = OUTER_MOMENTUM * momentum_ref[...] + average
    momentum_out[...] = new_momentum
    fragment_out[...] = params_ref[...] - OUTER_RATE * (average + OUTER_MOMENTUM * new_momentum)

    inv = own_columns[:, 0:1]
    total = jnp.zeros((rows, 1), f32)
    for k in [0] + order[::-1]:
        s = slot[k]
        if k:
            dx_copies[k].wait_recv()
        arrived = (dx_recv if k else dx_send)[s].astype(f32)
        grad_hat = arrived * modulated(own_columns, mod_ref[:, columns(k)])
        normed = x_ref[:, columns(k)].astype(f32) * inv
        total = total + jnp.sum(grad_hat * normed, axis=-1, keepdims=True)
        dx_sum[s * rows : (s + 1) * rows, :] = grad_hat
    mean = total / (n * part)
    for k in range(n):
        s = slot[k]
        normed = x_ref[:, columns(k)].astype(f32) * inv
        grad_ref[:, columns(k)] = (
            inv * (dx_sum[s * rows : (s + 1) * rows, :] - normed * mean)
        ).astype(bf16)

    for copies in (x_copies, side_copies, line_copies, gather_line, gather_pair, dx_copies):
        for copy in copies.values():
            copy.wait_send()
    for copy in pair_copies + outer_copies:
        copy.wait_send()
    for copy in dw_copies[-2:]:
        copy.wait()


def shards(
    clip_tokens,
    frame_ids,
    modulation,
    query_gain,
    query_weight,
    query_cotangent,
    pseudo_grad,
    outer_params,
    outer_momentum,
):
    n = lax.axis_size("fsdp")
    replicas = lax.axis_size("rep")
    rows, width = clip_tokens.shape
    part = width // n
    columns = query_weight.shape[2]
    chunk = columns // CHUNKS
    half = n // 2
    head = query_gain.shape[0]
    entries = outer_params.shape[0]
    fold = (entries // 128, 128)
    vmem = pl.BlockSpec(memory_space=pltpu.VMEM)
    hbm = pl.BlockSpec(memory_space=pl.ANY)
    dma = pltpu.SemaphoreType.DMA
    shape = jax.ShapeDtypeStruct
    outs = pl.pallas_call(
        functools.partial(kernel, n, replicas),
        out_shape=(
            shape((rows, width), bf16),
            shape((part, columns), bf16),
            shape((modulation.shape[0], part), f32),
            shape(fold, f32),
            shape(fold, f32),
        ),
        in_specs=[vmem] * 4 + [hbm] * 2 + [vmem] * 3,
        out_specs=(vmem, hbm, vmem, vmem, vmem),
        scratch_shapes=[
            pltpu.VMEM((part, columns), bf16),
            pltpu.VMEM((rows, columns), bf16),
            pltpu.VMEM((n, 8, rows), f32),
            pltpu.VMEM((n, rows, part), bf16),
            pltpu.VMEM((n, rows, part), bf16),
            pltpu.VMEM((part, n * rows), bf16),
            pltpu.VMEM((CHUNKS, half, rows, chunk), bf16),
            pltpu.VMEM((CHUNKS, half, rows, chunk), bf16),
            pltpu.VMEM((CHUNKS, half, rows, chunk), bf16),
            pltpu.VMEM((CHUNKS, half - 1, rows, chunk), bf16),
            pltpu.VMEM((2, rows, chunk), f32),
            pltpu.VMEM((CHUNKS, 2, half, rows, chunk), bf16),
            pltpu.VMEM((2, part, chunk), bf16),
            pltpu.VMEM((n * rows, part), f32),
            pltpu.VMEM((n, rows, part), bf16),
            pltpu.VMEM(fold, bf16),
            pltpu.VMEM((replicas - 1, *fold), bf16),
            dma((2,)),
            dma((CHUNKS,)),
            dma((2, replicas - 1)),
            dma((2, n)),
            dma((2, n)),
            dma((2, CHUNKS)),
            dma((2, CHUNKS, half)),
            dma((2, CHUNKS, half)),
            dma((2, CHUNKS, half)),
            dma((2, n)),
        ],
        compiler_params=pltpu.CompilerParams(
            collective_id=0, has_side_effects=True, vmem_limit_bytes=60 * 2**20
        ),
    )(
        clip_tokens,
        frame_ids.reshape(1, rows),
        modulation,
        query_gain.reshape(1, head),
        query_weight[0],
        query_cotangent,
        pseudo_grad.reshape(fold),
        outer_params.reshape(fold),
        outer_momentum.reshape(fold),
    )
    input_grad, weight_grad, table_grad, new_fragment, new_momentum = outs
    return (
        input_grad,
        weight_grad[None],
        table_grad[None],
        new_fragment.reshape(entries),
        new_momentum.reshape(entries),
    )


def solution(mesh):
    placed = (
        P(("rep", "fsdp"), None),
        P(("rep", "fsdp")),
        P(),
        P(),
        P("rep", "fsdp", None),
        P(("rep", "fsdp"), None),
        P("rep", "fsdp"),
        P("fsdp"),
        P("fsdp"),
    )
    return jax.shard_map(
        shards,
        mesh=mesh,
        in_specs=placed,
        out_specs=(
            P(("rep", "fsdp"), None),
            P("rep", "fsdp", None),
            P("rep", None, "fsdp"),
            P("fsdp"),
            P("fsdp"),
        ),
        check_vma=False,
    )
```

```python
import functools

import jax
import jax.numpy as jnp
from jax import lax
from jax.experimental import pallas as pl
from jax.experimental.pallas import tpu as pltpu
from jax.sharding import PartitionSpec as P

EPSILON = 1e-06
OUTER_RATE = 0.7
OUTER_MOMENTUM = 0.9
CHUNKS = 4
TILE = 256
MESH = pl.DeviceIdType.MESH
EXACT = lax.Precision.HIGHEST
f32 = jnp.float32
bf16 = jnp.bfloat16


def partner(index, offset):
    bit = 1
    moved = index
    while bit <= offset:
        if offset & bit:
            moved = moved + bit * (1 - 2 * ((index // bit) % 2))
        bit *= 2
    return moved


def kernel(
    n,
    replicas,
    x_ref,
    frames_ref,
    mod_ref,
    gain_ref,
    w_hbm,
    cot_hbm,
    pseudo_ref,
    params_ref,
    momentum_ref,
    grad_ref,
    dw_hbm,
    table_ref,
    fragment_out,
    momentum_out,
    w_vmem,
    cot_vmem,
    sides,
    side_cols,
    x_all,
    ni,
    ni_t,
    p_send,
    p_keep,
    p_pair,
    p_line,
    p_own,
    gathered,
    dw_vmem,
    scales,
    dx_recv,
    outer_send,
    outer_recv,
    local_sem,
    dw_sem,
    outer_sem,
    x_sem,
    side_sem,
    pair_sem,
    line_sem,
    gather_line_sem,
    gather_pair_sem,
    dx_sem,
):
    dx_send = ni
    me = lax.axis_index("fsdp")
    rep = lax.axis_index("rep")
    half = n // 2
    rows = x_ref.shape[0]
    part = x_ref.shape[1] // n
    chunk = w_vmem.shape[1] // CHUNKS
    head = gain_ref.shape[1]
    frame_count = mod_ref.shape[0]
    at = [partner(me, k) for k in range(n)]
    slot = [(k % 2) * half + k // 2 for k in range(n)]

    def send(src, dst, sems, where, k):
        return pltpu.make_async_remote_copy(
            src_ref=src,
            dst_ref=dst,
            send_sem=sems.at[(0, *where)],
            recv_sem=sems.at[(1, *where)],
            device_id={"fsdp": at[k]},
            device_id_type=MESH,
        )

    def columns(k):
        return pl.ds(pl.multiple_of(at[k] * part, 128), part)

    load_w = pltpu.make_async_copy(w_hbm, w_vmem, local_sem.at[0])
    load_cot = pltpu.make_async_copy(cot_hbm, cot_vmem, local_sem.at[1])
    load_w.start()
    load_cot.start()
    outer_send[...] = pseudo_ref[...].astype(bf16)

    barrier = pltpu.get_barrier_semaphore()
    for k in range(1, n):
        pl.semaphore_signal(barrier, inc=1, device_id={"fsdp": at[k]}, device_id_type=MESH)
    for k in range(1, replicas):
        pl.semaphore_signal(
            barrier, inc=1, device_id={"rep": partner(rep, k)}, device_id_type=MESH
        )
    pl.semaphore_wait(barrier, n + replicas - 2)

    order = sorted(range(1, n), key=lambda k: -k)
    part_rows = rows // CHUNKS
    spans = [pl.ds(c * part_rows, part_rows) for c in range(CHUNKS)]
    x_copies, dx_copies = {}, {}

    def send_tokens(c):
        for k in order:
            x_copies[c, k] = send(
                x_ref.at[spans[c], columns(k)], x_all.at[slot[k], spans[c]], x_sem, (c, k), k
            )
            x_copies[c, k].start()

    send_tokens(0)
    send_tokens(1)

    x_f = x_ref[...].astype(f32)
    inverse = lax.rsqrt(jnp.mean(x_f * x_f, axis=-1, keepdims=True) + EPSILON)
    lane = lax.broadcasted_iota(jnp.int32, (rows, rows), 1)
    row = lax.broadcasted_iota(jnp.int32, (rows, rows), 0)
    eye = (lane == row).astype(f32)
    contract_last = (((1,), (1,)), ((), ()))
    inverse_row = jnp.sum(eye * inverse, axis=0, keepdims=True)
    side_row = lax.broadcasted_iota(jnp.int32, (8, rows), 0)
    sides[0] = jnp.where(side_row == 0, inverse_row, frames_ref[...].astype(f32))
    side_copies = {}
    for k in order:
        side_copies[k] = send(sides.at[0], sides.at[slot[k]], side_sem, (k,), k)
        side_copies[k].start()

    outer_copies = []
    for k in range(1, replicas):
        copy = pltpu.make_async_remote_copy(
            src_ref=outer_send,
            dst_ref=outer_recv.at[k - 1],
            send_sem=outer_sem.at[0, k - 1],
            recv_sem=outer_sem.at[1, k - 1],
            device_id={"rep": partner(rep, k)},
            device_id_type=MESH,
        )
        copy.start()
        outer_copies.append(copy)

    def set_columns(s):
        side_cols[s] = lax.dot_general(
            eye, sides[s], contract_last, precision=EXACT, preferred_element_type=f32
        )

    def modulated(frames, block):
        lanes = lax.broadcasted_iota(jnp.int32, (frames.shape[0], frame_count), 1).astype(f32)
        one_hot = (frames == lanes).astype(f32)
        return 1.0 + jnp.dot(one_hot, block, precision=EXACT, preferred_element_type=f32)

    set_columns(0)
    for k in range(n):
        scales[slot[k]] = modulated(side_cols[0, :, 1:2], mod_ref[:, columns(k)])
    x_all[0] = x_ref[:, columns(0)]
    for k in order[::-1]:
        side_copies[k].wait_recv()
        set_columns(slot[k])
    load_w.wait()
    load_cot.wait()

    def tiles(total, body):
        size = TILE if total % TILE == 0 else TILE // 2
        lax.fori_loop(0, total // size, lambda j, carry: (body(j, size), carry)[1], 0)

    pair_copies = []

    def project_tokens(c):
        for k in order[::-1]:
            x_copies[c, k].wait_recv()
        if c + 2 < CHUNKS:
            send_tokens(c + 2)
        scale = modulated(
            side_cols[:, spans[c], 1:2].reshape(n * part_rows, 1), mod_ref[:, columns(0)]
        )
        normed = x_all[:, spans[c], :].astype(f32) * side_cols[:, spans[c], 0:1]
        ni[:, spans[c], :] = (normed * scale.reshape(n, part_rows, part)).astype(bf16)
        for kx, target in ((1, p_send), (0, p_keep)):

            def project(j, size, kx=kx, target=target):
                span = pl.ds(pl.multiple_of(j * size, size), size)
                left = ni[kx * half : (kx + 1) * half, spans[c], :].reshape(half * part_rows, part)
                value = jnp.dot(left, w_vmem[:, span], preferred_element_type=f32).astype(bf16)
                target[c, :, :, span] = value.reshape(half, part_rows, size)

            tiles(w_vmem.shape[1], project)
            if kx == 1:
                copy = send(p_send.at[c], p_pair.at[c], pair_sem, (c,), 1)
                copy.start()
                pair_copies.append(copy)

    line_copies, gather_line, gather_pair = {}, {}, {}

    def reduce_pair(c):
        pair_copies[c].wait_recv()
        for kz in list(range(1, half))[::-1]:
            p_keep[c, kz] = (p_keep[c, kz].astype(f32) + p_pair[c, kz].astype(f32)).astype(bf16)
            line_copies[c, kz] = send(
                p_keep.at[c, kz], p_line.at[c, kz - 1], line_sem, (c, kz), 2 * kz
            )
            line_copies[c, kz].start()
        p_own[c % 2] = p_keep[c, 0].astype(f32) + p_pair[c, 0].astype(f32)

    def head_grads(c):
        for kz in range(1, half):
            line_copies[c, kz].wait_recv()
        gain = gain_ref[...]
        for h in range(w_vmem.shape[1] // head):
            span = slice(h * head, (h + 1) * head)
            projected = p_own[c % 2, :, span]
            for kz in range(1, half):
                projected = projected + p_line[c, kz - 1, :, span].astype(f32)
            head_inv = lax.rsqrt(
                jnp.mean(projected * projected, axis=-1, keepdims=True) + EPSILON
            )
            head_hat = projected * head_inv
            scaled = cot_vmem[spans[c], span].astype(f32) * gain
            mean = jnp.mean(scaled * head_hat, axis=-1, keepdims=True)
            gathered[0, 0, spans[c], span] = (head_inv * (scaled - head_hat * mean)).astype(bf16)
        own = gathered.at[0, 0, spans[c]]
        for kz in list(range(1, half))[::-1]:
            gather_line[c, kz] = send(
                own, gathered.at[0, kz, spans[c]], gather_line_sem, (c, kz), 2 * kz
            )
            gather_line[c, kz].start()
        gather_pair[c, 0] = send(own, gathered.at[1, 0, spans[c]], gather_pair_sem, (c, 0), 1)
        gather_pair[c, 0].start()

    def forward(c):
        for kz in range(1, half):
            gather_line[c, kz].wait_recv()
            gather_pair[c, kz] = send(
                gathered.at[0, kz, spans[c]],
                gathered.at[1, kz, spans[c]],
                gather_pair_sem,
                (c, kz),
                1,
            )
            gather_pair[c, kz].start()

    def feature(c):
        for kz in range(half):
            gather_pair[c, kz].wait_recv()

        def body(j, size):
            span = pl.ds(pl.multiple_of(j * size, size), size)
            g = gathered[:, :, spans[c], :].reshape(n * part_rows, w_vmem.shape[1])
            value = lax.dot_general(g, w_vmem[span, :], contract_last, preferred_element_type=f32)
            dx_send[:, spans[c], span] = value.astype(bf16).reshape(n, part_rows, size)

        tiles(part, body)
        for k in order:
            dx_copies[c, k] = send(
                dx_send.at[slot[k], spans[c]], dx_recv.at[slot[k], spans[c]], dx_sem, (c, k), k
            )
            dx_copies[c, k].start()

    dw_copies = []

    def weight(c):
        if c >= 2:
            dw_copies[c - 2].wait()
        span = slice(c * chunk, (c + 1) * chunk)

        def body(j, size):
            lines = pl.ds(pl.multiple_of(j * size, size), size)
            g = gathered[:, :, :, span].reshape(n * rows, chunk)
            dw_vmem[c % 2, lines, :] = jnp.dot(
                ni_t[lines, :], g, preferred_element_type=f32
            ).astype(bf16)

        tiles(part, body)
        copy = pltpu.make_async_copy(dw_vmem.at[c % 2], dw_hbm.at[:, span], dw_sem.at[c])
        copy.start()
        dw_copies.append(copy)

    def finish(c):
        inv = side_cols[0, spans[c], 0:1]
        total = jnp.zeros((part_rows, 1), f32)
        for k in [0] + order[::-1]:
            s = slot[k]
            if k:
                dx_copies[c, k].wait_recv()
            arrived = (dx_recv if k else dx_send)[s, spans[c], :].astype(f32)
            grad_hat = arrived * scales[s, spans[c], :]
            normed = x_ref[spans[c], columns(k)].astype(f32) * inv
            total = total + jnp.sum(grad_hat * normed, axis=-1, keepdims=True)
            scales[s, spans[c], :] = grad_hat
        mean = total / (n * part)
        for k in range(n):
            normed = x_ref[spans[c], columns(k)].astype(f32) * inv
            grad_ref[spans[c], columns(k)] = (
                inv * (scales[slot[k], spans[c], :] - normed * mean)
            ).astype(bf16)

    def outer_step():
        for copy in outer_copies:
            copy.wait_recv()
        terms = [outer_send[...].astype(f32)] + [
            outer_recv[k - 1].astype(f32) for k in range(1, replicas)
        ]
        while len(terms) > 1:
            terms = [terms[i] + terms[i + 1] for i in range(0, len(terms), 2)]
        average = terms[0] / replicas
        new_momentum = OUTER_MOMENTUM * momentum_ref[...] + average
        momentum_out[...] = new_momentum
        fragment_out[...] = params_ref[...] - OUTER_RATE * (
            average + OUTER_MOMENTUM * new_momentum
        )

    def table():
        frame_row = lax.broadcasted_iota(jnp.int32, (frame_count, rows), 0).astype(f32)
        summed = jnp.zeros((frame_count, part), f32)
        for s in range(n):
            normed = x_all[s].astype(f32) * side_cols[s, :, 0:1]
            picked = (sides[s, 1:2, :] == frame_row).astype(f32)
            summed = summed + jnp.dot(
                picked,
                dx_send[s].astype(f32) * normed,
                precision=EXACT,
                preferred_element_type=f32,
            )
        table_ref[...] = summed

    for t in range(CHUNKS + 4):
        if t < CHUNKS:
            project_tokens(t)
        if t == CHUNKS - 1:
            for s in range(n):
                ni_t[:, s * rows : (s + 1) * rows] = ni[s].astype(f32).T.astype(bf16)
        if 0 <= t - 1 < CHUNKS:
            reduce_pair(t - 1)
        if t == CHUNKS:
            outer_step()
        if 0 <= t - 2 < CHUNKS:
            head_grads(t - 2)
        if 0 <= t - 3 < CHUNKS:
            forward(t - 3)
        if 0 <= t - 4 < CHUNKS:
            feature(t - 4)
    for c in range(CHUNKS):
        weight(c)
        if c < CHUNKS - 1:
            finish(c)
    table()
    finish(CHUNKS - 1)

    for copies in (x_copies, side_copies, line_copies, gather_line, gather_pair, dx_copies):
        for copy in copies.values():
            copy.wait_send()
    for copy in pair_copies + outer_copies:
        copy.wait_send()
    for copy in dw_copies[-2:]:
        copy.wait()


def shards(
    clip_tokens,
    frame_ids,
    modulation,
    query_gain,
    query_weight,
    query_cotangent,
    pseudo_grad,
    outer_params,
    outer_momentum,
):
    n = lax.axis_size("fsdp")
    replicas = lax.axis_size("rep")
    rows, width = clip_tokens.shape
    part = width // n
    columns = query_weight.shape[2]
    chunk = columns // CHUNKS
    part_rows = rows // CHUNKS
    half = n // 2
    head = query_gain.shape[0]
    entries = outer_params.shape[0]
    fold = (entries // 128, 128)
    vmem = pl.BlockSpec(memory_space=pltpu.VMEM)
    hbm = pl.BlockSpec(memory_space=pl.ANY)
    dma = pltpu.SemaphoreType.DMA
    shape = jax.ShapeDtypeStruct
    outs = pl.pallas_call(
        functools.partial(kernel, n, replicas),
        out_shape=(
            shape((rows, width), bf16),
            shape((part, columns), bf16),
            shape((modulation.shape[0], part), f32),
            shape(fold, f32),
            shape(fold, f32),
        ),
        in_specs=[vmem] * 4 + [hbm] * 2 + [vmem] * 3,
        out_specs=(vmem, hbm, vmem, vmem, vmem),
        scratch_shapes=[
            pltpu.VMEM((part, columns), bf16),
            pltpu.VMEM((rows, columns), bf16),
            pltpu.VMEM((n, 8, rows), f32),
            pltpu.VMEM((n, rows, 8), f32),
            pltpu.VMEM((n, rows, part), bf16),
            pltpu.VMEM((n, rows, part), bf16),
            pltpu.VMEM((part, n * rows), bf16),
            pltpu.VMEM((CHUNKS, half, part_rows, columns), bf16),
            pltpu.VMEM((CHUNKS, half, part_rows, columns), bf16),
            pltpu.VMEM((CHUNKS, half, part_rows, columns), bf16),
            pltpu.VMEM((CHUNKS, half - 1, part_rows, columns), bf16),
            pltpu.VMEM((2, part_rows, columns), f32),
            pltpu.VMEM((2, half, rows, columns), bf16),
            pltpu.VMEM((2, part, chunk), bf16),
            pltpu.VMEM((n, rows, part), f32),
            pltpu.VMEM((n, rows, part), bf16),
            pltpu.VMEM(fold, bf16),
            pltpu.VMEM((replicas - 1, *fold), bf16),
            dma((2,)),
            dma((CHUNKS,)),
            dma((2, replicas - 1)),
            dma((2, CHUNKS, n)),
            dma((2, n)),
            dma((2, CHUNKS)),
            dma((2, CHUNKS, half)),
            dma((2, CHUNKS, half)),
            dma((2, CHUNKS, half)),
            dma((2, CHUNKS, n)),
        ],
        compiler_params=pltpu.CompilerParams(
            collective_id=0, has_side_effects=True, vmem_limit_bytes=62 * 2**20
        ),
    )(
        clip_tokens,
        frame_ids.reshape(1, rows),
        modulation,
        query_gain.reshape(1, head),
        query_weight[0],
        query_cotangent,
        pseudo_grad.reshape(fold),
        outer_params.reshape(fold),
        outer_momentum.reshape(fold),
    )
    input_grad, weight_grad, table_grad, new_fragment, new_momentum = outs
    return (
        input_grad,
        weight_grad[None],
        table_grad[None],
        new_fragment.reshape(entries),
        new_momentum.reshape(entries),
    )


def solution(mesh):
    placed = (
        P(("rep", "fsdp"), None),
        P(("rep", "fsdp")),
        P(),
        P(),
        P("rep", "fsdp", None),
        P(("rep", "fsdp"), None),
        P("rep", "fsdp"),
        P("fsdp"),
        P("fsdp"),
    )
    return jax.shard_map(
        shards,
        mesh=mesh,
        in_specs=placed,
        out_specs=(
            P(("rep", "fsdp"), None),
            P("rep", "fsdp", None),
            P("rep", None, "fsdp"),
            P("fsdp"),
            P("fsdp"),
        ),
        check_vma=False,
    )
```

```python
import functools

import jax
import jax.numpy as jnp
from jax import lax
from jax.experimental import pallas as pl
from jax.experimental.pallas import tpu as pltpu
from jax.sharding import PartitionSpec as P

EPSILON = 1e-06
OUTER_RATE = 0.7
OUTER_MOMENTUM = 0.9
CHUNKS = 4
TILE = 256
MESH = pl.DeviceIdType.MESH
EXACT = lax.Precision.HIGHEST
f32 = jnp.float32
bf16 = jnp.bfloat16


def partner(index, offset):
    bit = 1
    moved = index
    while bit <= offset:
        if offset & bit:
            moved = moved + bit * (1 - 2 * ((index // bit) % 2))
        bit *= 2
    return moved


def kernel(
    n,
    replicas,
    x_ref,
    frames_ref,
    mod_ref,
    gain_ref,
    w_hbm,
    cot_hbm,
    pseudo_ref,
    params_ref,
    momentum_ref,
    grad_ref,
    dw_hbm,
    table_ref,
    fragment_out,
    momentum_out,
    w_vmem,
    cot_vmem,
    sides,
    side_cols,
    x_all,
    ni,
    ni_t,
    p_send,
    p_keep,
    p_pair,
    p_line,
    p_own,
    gathered,
    dw_vmem,
    scales,
    dx_recv,
    outer_send,
    outer_recv,
    local_sem,
    dw_sem,
    outer_sem,
    x_sem,
    side_sem,
    pair_sem,
    line_sem,
    gather_line_sem,
    gather_pair_sem,
    pass_sem,
    dx_sem,
):
    dx_send = ni
    me = lax.axis_index("fsdp")
    rep = lax.axis_index("rep")
    half = n // 2
    rows = x_ref.shape[0]
    part = x_ref.shape[1] // n
    chunk = w_vmem.shape[1] // CHUNKS
    head = gain_ref.shape[1]
    frame_count = mod_ref.shape[0]
    at = [partner(me, k) for k in range(n)]
    slot = [(k % 2) * half + k // 2 for k in range(n)]

    def send(src, dst, sems, where, k):
        return pltpu.make_async_remote_copy(
            src_ref=src,
            dst_ref=dst,
            send_sem=sems.at[(0, *where)],
            recv_sem=sems.at[(1, *where)],
            device_id={"fsdp": at[k]},
            device_id_type=MESH,
        )

    def columns(k):
        return pl.ds(pl.multiple_of(at[k] * part, 128), part)

    load_w = pltpu.make_async_copy(w_hbm, w_vmem, local_sem.at[0])
    load_cot = pltpu.make_async_copy(cot_hbm, cot_vmem, local_sem.at[1])
    load_w.start()
    load_cot.start()
    outer_send[...] = pseudo_ref[...].astype(bf16)

    barrier = pltpu.get_barrier_semaphore()
    for k in range(1, n):
        pl.semaphore_signal(barrier, inc=1, device_id={"fsdp": at[k]}, device_id_type=MESH)
    for k in range(1, replicas):
        pl.semaphore_signal(
            barrier, inc=1, device_id={"rep": partner(rep, k)}, device_id_type=MESH
        )
    pl.semaphore_wait(barrier, n + replicas - 2)

    order = sorted(range(1, n), key=lambda k: -k)
    part_rows = rows // CHUNKS
    spans = [pl.ds(c * part_rows, part_rows) for c in range(CHUNKS)]
    x_copies, dx_copies = {}, {}

    def send_tokens(c):
        for k in order:
            x_copies[c, k] = send(
                x_ref.at[spans[c], columns(k)], x_all.at[slot[k], spans[c]], x_sem, (c, k), k
            )
            x_copies[c, k].start()

    send_tokens(0)
    send_tokens(1)

    x_f = x_ref[...].astype(f32)
    inverse = lax.rsqrt(jnp.mean(x_f * x_f, axis=-1, keepdims=True) + EPSILON)
    lane = lax.broadcasted_iota(jnp.int32, (rows, rows), 1)
    row = lax.broadcasted_iota(jnp.int32, (rows, rows), 0)
    eye = (lane == row).astype(f32)
    contract_last = (((1,), (1,)), ((), ()))
    inverse_row = jnp.sum(eye * inverse, axis=0, keepdims=True)
    side_row = lax.broadcasted_iota(jnp.int32, (8, rows), 0)
    sides[0] = jnp.where(side_row == 0, inverse_row, frames_ref[...].astype(f32))
    side_copies = {}
    for k in order:
        side_copies[k] = send(sides.at[0], sides.at[slot[k]], side_sem, (k,), k)
        side_copies[k].start()

    outer_copies = []
    for k in range(1, replicas):
        copy = pltpu.make_async_remote_copy(
            src_ref=outer_send,
            dst_ref=outer_recv.at[k - 1],
            send_sem=outer_sem.at[0, k - 1],
            recv_sem=outer_sem.at[1, k - 1],
            device_id={"rep": partner(rep, k)},
            device_id_type=MESH,
        )
        copy.start()
        outer_copies.append(copy)

    def set_columns(s):
        side_cols[s] = lax.dot_general(
            eye, sides[s], contract_last, precision=EXACT, preferred_element_type=f32
        )

    def modulated(frames, block):
        lanes = lax.broadcasted_iota(jnp.int32, (frames.shape[0], frame_count), 1).astype(f32)
        one_hot = (frames == lanes).astype(f32)
        return 1.0 + jnp.dot(one_hot, block, precision=EXACT, preferred_element_type=f32)

    set_columns(0)
    for k in range(n):
        scales[slot[k]] = modulated(side_cols[0, :, 1:2], mod_ref[:, columns(k)])
    x_all[0] = x_ref[:, columns(0)]
    for k in order[::-1]:
        side_copies[k].wait_recv()
        set_columns(slot[k])
    load_w.wait()
    load_cot.wait()

    def tiles(total, body):
        size = TILE if total % TILE == 0 else TILE // 2
        lax.fori_loop(0, total // size, lambda j, carry: (body(j, size), carry)[1], 0)

    passed_on = half == 4
    inner = (me // 2 + 1) // 2 == 1
    passes = {}
    pair_copies = []

    def project_tokens(c):
        for k in order[::-1]:
            x_copies[c, k].wait_recv()
        if c + 2 < CHUNKS:
            send_tokens(c + 2)
        scale = modulated(
            side_cols[:, spans[c], 1:2].reshape(n * part_rows, 1), mod_ref[:, columns(0)]
        )
        normed = x_all[:, spans[c], :].astype(f32) * side_cols[:, spans[c], 0:1]
        ni[:, spans[c], :] = (normed * scale.reshape(n, part_rows, part)).astype(bf16)
        for kx, target in ((1, p_send), (0, p_keep)):

            def project(j, size, kx=kx, target=target):
                span = pl.ds(pl.multiple_of(j * size, size), size)
                left = ni[kx * half : (kx + 1) * half, spans[c], :].reshape(half * part_rows, part)
                value = jnp.dot(left, w_vmem[:, span], preferred_element_type=f32).astype(bf16)
                target[c, :, :, span] = value.reshape(half, part_rows, size)

            tiles(w_vmem.shape[1], project)
            if kx == 1:
                copy = send(p_send.at[c], p_pair.at[c], pair_sem, (c,), 1)
                copy.start()
                pair_copies.append(copy)

    line_copies, gather_line, gather_pair = {}, {}, {}

    def reduce_pair(c):
        pair_copies[c].wait_recv()
        for kz in list(range(1, half))[::-1]:
            p_keep[c, kz] = (p_keep[c, kz].astype(f32) + p_pair[c, kz].astype(f32)).astype(bf16)
            line_copies[c, kz] = send(
                p_keep.at[c, kz], p_line.at[c, kz - 1], line_sem, (c, kz), 2 * kz
            )
            line_copies[c, kz].start()
        p_own[c % 2] = p_keep[c, 0].astype(f32) + p_pair[c, 0].astype(f32)

    def head_grads(c):
        for kz in range(1, half):
            line_copies[c, kz].wait_recv()
        gain = gain_ref[...]
        for h in range(w_vmem.shape[1] // head):
            span = slice(h * head, (h + 1) * head)
            projected = p_own[c % 2, :, span]
            for kz in range(1, half):
                projected = projected + p_line[c, kz - 1, :, span].astype(f32)
            head_inv = lax.rsqrt(
                jnp.mean(projected * projected, axis=-1, keepdims=True) + EPSILON
            )
            head_hat = projected * head_inv
            scaled = cot_vmem[spans[c], span].astype(f32) * gain
            mean = jnp.mean(scaled * head_hat, axis=-1, keepdims=True)
            gathered[0, 0, spans[c], span] = (head_inv * (scaled - head_hat * mean)).astype(bf16)
        own = gathered.at[0, 0, spans[c]]
        for kz in list(range(1, half))[::-1]:
            source = gathered.at[0, 1, spans[c]] if passed_on and kz == 2 else own
            target = 3 if passed_on and kz == 2 else kz
            gather_line[c, kz] = send(
                source, gathered.at[0, kz, spans[c]], gather_line_sem, (c, kz), 2 * target
            )
            if not passed_on or kz == 1:
                gather_line[c, kz].start()
        if passed_on:
            pl.when(inner)(gather_line[c, 3].start)
            for i, kz in enumerate((3, 2)):
                passes[c, i] = pltpu.make_async_remote_copy(
                    src_ref=gathered.at[0, kz, spans[c]],
                    dst_ref=gathered.at[0, 5 - kz, spans[c]],
                    send_sem=pass_sem.at[c, i],
                    recv_sem=gather_line_sem.at[1, c, 5 - kz],
                    device_id={"fsdp": at[2]},
                    device_id_type=MESH,
                )
        gather_pair[c, 0] = send(own, gathered.at[1, 0, spans[c]], gather_pair_sem, (c, 0), 1)
        gather_pair[c, 0].start()

    def pair_forward(c, kz):
        if (c, kz) not in gather_pair:
            gather_pair[c, kz] = send(
                gathered.at[0, kz, spans[c]],
                gathered.at[1, kz, spans[c]],
                gather_pair_sem,
                (c, kz),
                1,
            )
        gather_pair[c, kz].start()

    def forward(c, stage):
        if not passed_on:
            if stage == 0:
                for kz in range(1, half):
                    gather_line[c, kz].wait_recv()
                    pair_forward(c, kz)
            return

        if stage == 0:
            gather_line[c, 1].wait_recv()

            @pl.when(inner)
            def pass_first():
                gather_line[c, 2].start()

            pair_forward(c, 1)
            gather_pair[c, 3] = send(
                gathered.at[0, 3, spans[c]],
                gathered.at[1, 3, spans[c]],
                gather_pair_sem,
                (c, 3),
                1,
            )

            @pl.when(inner)
            def pass_second():
                gather_line[c, 3].wait_recv()
                passes[c, 0].start()
                gather_pair[c, 3].start()

        if stage == 1:
            gather_line[c, 2].wait_recv()
            pl.when(inner)(passes[c, 1].start)
            pair_forward(c, 2)

        if stage == 2:

            @pl.when(jnp.logical_not(inner))
            def last():
                gather_line[c, 3].wait_recv()
                gather_pair[c, 3].start()

    def feature(c):
        for kz in range(half):
            gather_pair[c, kz].wait_recv()

        def body(j, size):
            span = pl.ds(pl.multiple_of(j * size, size), size)
            g = gathered[:, :, spans[c], :].reshape(n * part_rows, w_vmem.shape[1])
            value = lax.dot_general(g, w_vmem[span, :], contract_last, preferred_element_type=f32)
            dx_send[:, spans[c], span] = value.astype(bf16).reshape(n, part_rows, size)

        tiles(part, body)
        for k in order:
            dx_copies[c, k] = send(
                dx_send.at[slot[k], spans[c]], dx_recv.at[slot[k], spans[c]], dx_sem, (c, k), k
            )
            dx_copies[c, k].start()

    dw_copies = []

    def weight(c):
        if c >= 2:
            dw_copies[c - 2].wait()
        span = slice(c * chunk, (c + 1) * chunk)

        def body(j, size):
            lines = pl.ds(pl.multiple_of(j * size, size), size)
            g = gathered[:, :, :, span].reshape(n * rows, chunk)
            dw_vmem[c % 2, lines, :] = jnp.dot(
                ni_t[lines, :], g, preferred_element_type=f32
            ).astype(bf16)

        tiles(part, body)
        copy = pltpu.make_async_copy(dw_vmem.at[c % 2], dw_hbm.at[:, span], dw_sem.at[c])
        copy.start()
        dw_copies.append(copy)

    def finish(c):
        inv = side_cols[0, spans[c], 0:1]
        total = jnp.zeros((part_rows, 1), f32)
        for k in [0] + order[::-1]:
            s = slot[k]
            if k:
                dx_copies[c, k].wait_recv()
            arrived = (dx_recv if k else dx_send)[s, spans[c], :].astype(f32)
            grad_hat = arrived * scales[s, spans[c], :]
            normed = x_ref[spans[c], columns(k)].astype(f32) * inv
            total = total + jnp.sum(grad_hat * normed, axis=-1, keepdims=True)
            scales[s, spans[c], :] = grad_hat
        mean = total / (n * part)
        for k in range(n):
            normed = x_ref[spans[c], columns(k)].astype(f32) * inv
            grad_ref[spans[c], columns(k)] = (
                inv * (scales[slot[k], spans[c], :] - normed * mean)
            ).astype(bf16)

    def outer_step():
        for copy in outer_copies:
            copy.wait_recv()
        terms = [outer_send[...].astype(f32)] + [
            outer_recv[k - 1].astype(f32) for k in range(1, replicas)
        ]
        while len(terms) > 1:
            terms = [terms[i] + terms[i + 1] for i in range(0, len(terms), 2)]
        average = terms[0] / replicas
        new_momentum = OUTER_MOMENTUM * momentum_ref[...] + average
        momentum_out[...] = new_momentum
        fragment_out[...] = params_ref[...] - OUTER_RATE * (
            average + OUTER_MOMENTUM * new_momentum
        )

    def table():
        frame_row = lax.broadcasted_iota(jnp.int32, (frame_count, rows), 0).astype(f32)
        summed = jnp.zeros((frame_count, part), f32)
        for s in range(n):
            normed = x_all[s].astype(f32) * side_cols[s, :, 0:1]
            picked = (sides[s, 1:2, :] == frame_row).astype(f32)
            summed = summed + jnp.dot(
                picked,
                dx_send[s].astype(f32) * normed,
                precision=EXACT,
                preferred_element_type=f32,
            )
        table_ref[...] = summed

    for t in range(CHUNKS + 4):
        if t < CHUNKS:
            project_tokens(t)
        if t == CHUNKS - 1:
            for s in range(n):
                ni_t[:, s * rows : (s + 1) * rows] = ni[s].astype(f32).T.astype(bf16)
        ready = 0 <= t - 3 < CHUNKS
        if ready:
            forward(t - 3, 0)
        if 0 <= t - 1 < CHUNKS:
            reduce_pair(t - 1)
        if t == CHUNKS:
            outer_step()
        if ready:
            forward(t - 3, 1)
        if 0 <= t - 2 < CHUNKS:
            head_grads(t - 2)
        if ready:
            forward(t - 3, 2)
        if 0 <= t - 4 < CHUNKS:
            feature(t - 4)
    for c in range(CHUNKS):
        weight(c)
        if c < CHUNKS - 1:
            finish(c)
    table()
    finish(CHUNKS - 1)

    for copies in (x_copies, side_copies, line_copies, gather_pair, dx_copies):
        for copy in copies.values():
            copy.wait_send()
    for (c, kz), copy in gather_line.items():
        if not passed_on or kz == 1:
            copy.wait_send()
    if passed_on:

        @pl.when(inner)
        def sent():
            for c in range(CHUNKS):
                for copy in (gather_line[c, 2], gather_line[c, 3], passes[c, 0], passes[c, 1]):
                    copy.wait_send()

    for copy in pair_copies + outer_copies:
        copy.wait_send()
    for copy in dw_copies[-2:]:
        copy.wait()


def shards(
    clip_tokens,
    frame_ids,
    modulation,
    query_gain,
    query_weight,
    query_cotangent,
    pseudo_grad,
    outer_params,
    outer_momentum,
):
    n = lax.axis_size("fsdp")
    replicas = lax.axis_size("rep")
    rows, width = clip_tokens.shape
    part = width // n
    columns = query_weight.shape[2]
    chunk = columns // CHUNKS
    part_rows = rows // CHUNKS
    half = n // 2
    head = query_gain.shape[0]
    entries = outer_params.shape[0]
    fold = (entries // 128, 128)
    vmem = pl.BlockSpec(memory_space=pltpu.VMEM)
    hbm = pl.BlockSpec(memory_space=pl.ANY)
    dma = pltpu.SemaphoreType.DMA
    shape = jax.ShapeDtypeStruct
    outs = pl.pallas_call(
        functools.partial(kernel, n, replicas),
        out_shape=(
            shape((rows, width), bf16),
            shape((part, columns), bf16),
            shape((modulation.shape[0], part), f32),
            shape(fold, f32),
            shape(fold, f32),
        ),
        in_specs=[vmem] * 4 + [hbm] * 2 + [vmem] * 3,
        out_specs=(vmem, hbm, vmem, vmem, vmem),
        scratch_shapes=[
            pltpu.VMEM((part, columns), bf16),
            pltpu.VMEM((rows, columns), bf16),
            pltpu.VMEM((n, 8, rows), f32),
            pltpu.VMEM((n, rows, 8), f32),
            pltpu.VMEM((n, rows, part), bf16),
            pltpu.VMEM((n, rows, part), bf16),
            pltpu.VMEM((part, n * rows), bf16),
            pltpu.VMEM((CHUNKS, half, part_rows, columns), bf16),
            pltpu.VMEM((CHUNKS, half, part_rows, columns), bf16),
            pltpu.VMEM((CHUNKS, half, part_rows, columns), bf16),
            pltpu.VMEM((CHUNKS, half - 1, part_rows, columns), bf16),
            pltpu.VMEM((2, part_rows, columns), f32),
            pltpu.VMEM((2, half, rows, columns), bf16),
            pltpu.VMEM((2, part, chunk), bf16),
            pltpu.VMEM((n, rows, part), f32),
            pltpu.VMEM((n, rows, part), bf16),
            pltpu.VMEM(fold, bf16),
            pltpu.VMEM((replicas - 1, *fold), bf16),
            dma((2,)),
            dma((CHUNKS,)),
            dma((2, replicas - 1)),
            dma((2, CHUNKS, n)),
            dma((2, n)),
            dma((2, CHUNKS)),
            dma((2, CHUNKS, half)),
            dma((2, CHUNKS, half)),
            dma((2, CHUNKS, half)),
            dma((CHUNKS, 2)),
            dma((2, CHUNKS, n)),
        ],
        compiler_params=pltpu.CompilerParams(
            collective_id=0, has_side_effects=True, vmem_limit_bytes=62 * 2**20
        ),
    )(
        clip_tokens,
        frame_ids.reshape(1, rows),
        modulation,
        query_gain.reshape(1, head),
        query_weight[0],
        query_cotangent,
        pseudo_grad.reshape(fold),
        outer_params.reshape(fold),
        outer_momentum.reshape(fold),
    )
    input_grad, weight_grad, table_grad, new_fragment, new_momentum = outs
    return (
        input_grad,
        weight_grad[None],
        table_grad[None],
        new_fragment.reshape(entries),
        new_momentum.reshape(entries),
    )


def solution(mesh):
    placed = (
        P(("rep", "fsdp"), None),
        P(("rep", "fsdp")),
        P(),
        P(),
        P("rep", "fsdp", None),
        P(("rep", "fsdp"), None),
        P("rep", "fsdp"),
        P("fsdp"),
        P("fsdp"),
    )
    return jax.shard_map(
        shards,
        mesh=mesh,
        in_specs=placed,
        out_specs=(
            P(("rep", "fsdp"), None),
            P("rep", "fsdp", None),
            P("rep", None, "fsdp"),
            P("fsdp"),
            P("fsdp"),
        ),
        check_vma=False,
    )
```

```python
import functools

import jax
import jax.numpy as jnp
from jax import lax
from jax.experimental import pallas as pl
from jax.experimental.pallas import tpu as pltpu
from jax.sharding import PartitionSpec as P

EPSILON = 1e-06
OUTER_RATE = 0.7
OUTER_MOMENTUM = 0.9
CHUNKS = 4
TILE = 256
MESH = pl.DeviceIdType.MESH
EXACT = lax.Precision.HIGHEST
f32 = jnp.float32
bf16 = jnp.bfloat16


def partner(index, offset):
    bit = 1
    moved = index
    while bit <= offset:
        if offset & bit:
            moved = moved + bit * (1 - 2 * ((index // bit) % 2))
        bit *= 2
    return moved


def kernel(
    n,
    replicas,
    x_ref,
    frames_ref,
    mod_ref,
    gain_ref,
    w_hbm,
    cot_hbm,
    pseudo_ref,
    params_ref,
    momentum_ref,
    grad_ref,
    dw_hbm,
    table_ref,
    fragment_out,
    momentum_out,
    w_vmem,
    cot_vmem,
    sides,
    side_cols,
    x_all,
    ni,
    ni_t,
    p_send,
    p_keep,
    p_pair,
    p_line,
    cross,
    p_own,
    gathered,
    dw_vmem,
    scales,
    dx_recv,
    outer_send,
    outer_recv,
    local_sem,
    dw_sem,
    outer_sem,
    x_sem,
    side_sem,
    pair_sem,
    line_sem,
    cross_sem,
    gather_line_sem,
    gather_pair_sem,
    pass_sem,
    dx_sem,
):
    dx_send = ni
    me = lax.axis_index("fsdp")
    rep = lax.axis_index("rep")
    half = n // 2
    rows = x_ref.shape[0]
    part = x_ref.shape[1] // n
    chunk = w_vmem.shape[1] // CHUNKS
    head = gain_ref.shape[1]
    frame_count = mod_ref.shape[0]
    at = [partner(me, k) for k in range(n)]
    slot = [(k % 2) * half + k // 2 for k in range(n)]

    def send(src, dst, sems, where, k):
        return pltpu.make_async_remote_copy(
            src_ref=src,
            dst_ref=dst,
            send_sem=sems.at[(0, *where)],
            recv_sem=sems.at[(1, *where)],
            device_id={"fsdp": at[k]},
            device_id_type=MESH,
        )

    def columns(k):
        return pl.ds(pl.multiple_of(at[k] * part, 128), part)

    load_w = pltpu.make_async_copy(w_hbm, w_vmem, local_sem.at[0])
    load_cot = pltpu.make_async_copy(cot_hbm, cot_vmem, local_sem.at[1])
    load_w.start()
    load_cot.start()
    outer_send[...] = pseudo_ref[...].astype(bf16)

    barrier = pltpu.get_barrier_semaphore()
    for k in range(1, n):
        pl.semaphore_signal(barrier, inc=1, device_id={"fsdp": at[k]}, device_id_type=MESH)
    for k in range(1, replicas):
        pl.semaphore_signal(
            barrier, inc=1, device_id={"rep": partner(rep, k)}, device_id_type=MESH
        )
    pl.semaphore_wait(barrier, n + replicas - 2)

    order = sorted(range(1, n), key=lambda k: -k)
    part_rows = rows // CHUNKS
    spans = [pl.ds(c * part_rows, part_rows) for c in range(CHUNKS)]
    x_copies, dx_copies = {}, {}

    def send_tokens(c):
        for k in order:
            x_copies[c, k] = send(
                x_ref.at[spans[c], columns(k)], x_all.at[slot[k], spans[c]], x_sem, (c, k), k
            )
            x_copies[c, k].start()

    send_tokens(0)
    send_tokens(1)

    x_f = x_ref[...].astype(f32)
    inverse = lax.rsqrt(jnp.mean(x_f * x_f, axis=-1, keepdims=True) + EPSILON)
    lane = lax.broadcasted_iota(jnp.int32, (rows, rows), 1)
    row = lax.broadcasted_iota(jnp.int32, (rows, rows), 0)
    eye = (lane == row).astype(f32)
    contract_last = (((1,), (1,)), ((), ()))
    inverse_row = jnp.sum(eye * inverse, axis=0, keepdims=True)
    side_row = lax.broadcasted_iota(jnp.int32, (8, rows), 0)
    sides[0] = jnp.where(side_row == 0, inverse_row, frames_ref[...].astype(f32))
    side_copies = {}
    for k in order:
        side_copies[k] = send(sides.at[0], sides.at[slot[k]], side_sem, (k,), k)
        side_copies[k].start()

    outer_copies = []
    for k in range(1, replicas):
        copy = pltpu.make_async_remote_copy(
            src_ref=outer_send,
            dst_ref=outer_recv.at[k - 1],
            send_sem=outer_sem.at[0, k - 1],
            recv_sem=outer_sem.at[1, k - 1],
            device_id={"rep": partner(rep, k)},
            device_id_type=MESH,
        )
        copy.start()
        outer_copies.append(copy)

    def set_columns(s):
        side_cols[s] = lax.dot_general(
            eye, sides[s], contract_last, precision=EXACT, preferred_element_type=f32
        )

    def modulated(frames, block):
        lanes = lax.broadcasted_iota(jnp.int32, (frames.shape[0], frame_count), 1).astype(f32)
        one_hot = (frames == lanes).astype(f32)
        return 1.0 + jnp.dot(one_hot, block, precision=EXACT, preferred_element_type=f32)

    set_columns(0)
    for k in range(n):
        scales[slot[k]] = modulated(side_cols[0, :, 1:2], mod_ref[:, columns(k)])
    x_all[0] = x_ref[:, columns(0)]
    for k in order[::-1]:
        side_copies[k].wait_recv()
        set_columns(slot[k])
    load_w.wait()
    load_cot.wait()

    def tiles(total, body):
        size = TILE if total % TILE == 0 else TILE // 2
        lax.fori_loop(0, total // size, lambda j, carry: (body(j, size), carry)[1], 0)

    passed_on = half == 4
    inner = (me // 2 + 1) // 2 == 1
    passes, crossing = {}, {}
    pair_copies = []

    def project_tokens(c):
        for k in order[::-1]:
            x_copies[c, k].wait_recv()
        if c + 2 < CHUNKS:
            send_tokens(c + 2)
        scale = modulated(
            side_cols[:, spans[c], 1:2].reshape(n * part_rows, 1), mod_ref[:, columns(0)]
        )
        normed = x_all[:, spans[c], :].astype(f32) * side_cols[:, spans[c], 0:1]
        ni[:, spans[c], :] = (normed * scale.reshape(n, part_rows, part)).astype(bf16)
        for kx, target in ((1, p_send), (0, p_keep)):

            def project(j, size, kx=kx, target=target):
                span = pl.ds(pl.multiple_of(j * size, size), size)
                left = ni[kx * half : (kx + 1) * half, spans[c], :].reshape(half * part_rows, part)
                value = jnp.dot(left, w_vmem[:, span], preferred_element_type=f32).astype(bf16)
                target[c, :, :, span] = value.reshape(half, part_rows, size)

            tiles(w_vmem.shape[1], project)
            if kx == 1:
                copy = send(p_send.at[c], p_pair.at[c], pair_sem, (c,), 1)
                copy.start()
                pair_copies.append(copy)

    line_copies, gather_line, gather_pair = {}, {}, {}

    def reduce_pair(c):
        pair_copies[c].wait_recv()
        for kz in list(range(1, half))[::-1]:
            p_keep[c, kz] = (p_keep[c, kz].astype(f32) + p_pair[c, kz].astype(f32)).astype(bf16)
            line_copies[c, kz] = send(
                p_keep.at[c, kz],
                p_line.at[c, kz - 1],
                line_sem,
                (c, kz),
                2 if passed_on else 2 * kz,
            )
            if passed_on:
                pl.when(jnp.logical_not(inner))(line_copies[c, kz].start)
            else:
                line_copies[c, kz].start()
        if passed_on:
            for kz in (2, 3):
                crossing[c, kz] = send(
                    p_keep.at[c, kz], cross.at[c, kz - 2], cross_sem, (c, kz - 2), 6
                )
        p_own[c % 2] = p_keep[c, 0].astype(f32) + p_pair[c, 0].astype(f32)

    def add_keep(c, kz, other):
        p_keep[c, kz] = (p_keep[c, kz].astype(f32) + other.astype(f32)).astype(bf16)

    def reduce_line(c, stage):
        if not passed_on:
            return

        @pl.when(inner)
        def combine():
            if stage == 0:
                line_copies[c, 3].wait_recv()
                add_keep(c, 2, p_line[c, 2])
                crossing[c, 2].start()
                line_copies[c, 2].wait_recv()
                add_keep(c, 3, p_line[c, 1])
                crossing[c, 3].start()
                line_copies[c, 1].wait_recv()
                p_own[c % 2] = p_own[c % 2] + p_line[c, 0].astype(f32)
            else:
                crossing[c, 2].wait_recv()
                add_keep(c, 1, cross[c, 0])
                line_copies[c, 1].start()
                crossing[c, 3].wait_recv()
                p_own[c % 2] = p_own[c % 2] + cross[c, 1].astype(f32)

        if stage == 1:

            @pl.when(jnp.logical_not(inner))
            def arrive():
                line_copies[c, 1].wait_recv()
                p_own[c % 2] = p_own[c % 2] + p_line[c, 0].astype(f32)

    def head_grads(c):
        if not passed_on:
            for kz in range(1, half):
                line_copies[c, kz].wait_recv()
        gain = gain_ref[...]
        for h in range(w_vmem.shape[1] // head):
            span = slice(h * head, (h + 1) * head)
            projected = p_own[c % 2, :, span]
            for kz in range(1, 1 if passed_on else half):
                projected = projected + p_line[c, kz - 1, :, span].astype(f32)
            head_inv = lax.rsqrt(
                jnp.mean(projected * projected, axis=-1, keepdims=True) + EPSILON
            )
            head_hat = projected * head_inv
            scaled = cot_vmem[spans[c], span].astype(f32) * gain
            mean = jnp.mean(scaled * head_hat, axis=-1, keepdims=True)
            gathered[0, 0, spans[c], span] = (head_inv * (scaled - head_hat * mean)).astype(bf16)
        own = gathered.at[0, 0, spans[c]]
        for kz in list(range(1, half))[::-1]:
            source = gathered.at[0, 1, spans[c]] if passed_on and kz == 2 else own
            target = 3 if passed_on and kz == 2 else kz
            gather_line[c, kz] = send(
                source, gathered.at[0, kz, spans[c]], gather_line_sem, (c, kz), 2 * target
            )
            if not passed_on or kz == 1:
                gather_line[c, kz].start()
        if passed_on:
            pl.when(inner)(gather_line[c, 3].start)
            for i, kz in enumerate((3, 2)):
                passes[c, i] = pltpu.make_async_remote_copy(
                    src_ref=gathered.at[0, kz, spans[c]],
                    dst_ref=gathered.at[0, 5 - kz, spans[c]],
                    send_sem=pass_sem.at[c, i],
                    recv_sem=gather_line_sem.at[1, c, 5 - kz],
                    device_id={"fsdp": at[2]},
                    device_id_type=MESH,
                )
        gather_pair[c, 0] = send(own, gathered.at[1, 0, spans[c]], gather_pair_sem, (c, 0), 1)
        gather_pair[c, 0].start()

    def pair_forward(c, kz):
        if (c, kz) not in gather_pair:
            gather_pair[c, kz] = send(
                gathered.at[0, kz, spans[c]],
                gathered.at[1, kz, spans[c]],
                gather_pair_sem,
                (c, kz),
                1,
            )
        gather_pair[c, kz].start()

    def forward(c, stage):
        if not passed_on:
            if stage == 0:
                for kz in range(1, half):
                    gather_line[c, kz].wait_recv()
                    pair_forward(c, kz)
            return

        if stage == 0:
            gather_line[c, 1].wait_recv()

            @pl.when(inner)
            def pass_first():
                gather_line[c, 2].start()

            pair_forward(c, 1)
            gather_pair[c, 3] = send(
                gathered.at[0, 3, spans[c]],
                gathered.at[1, 3, spans[c]],
                gather_pair_sem,
                (c, 3),
                1,
            )

            @pl.when(inner)
            def pass_second():
                gather_line[c, 3].wait_recv()
                passes[c, 0].start()
                gather_pair[c, 3].start()

        if stage == 1:
            gather_line[c, 2].wait_recv()
            pl.when(inner)(passes[c, 1].start)
            pair_forward(c, 2)

        if stage == 2:

            @pl.when(jnp.logical_not(inner))
            def last():
                gather_line[c, 3].wait_recv()
                gather_pair[c, 3].start()

    def feature(c):
        for kz in range(half):
            gather_pair[c, kz].wait_recv()

        def body(j, size):
            span = pl.ds(pl.multiple_of(j * size, size), size)
            g = gathered[:, :, spans[c], :].reshape(n * part_rows, w_vmem.shape[1])
            value = lax.dot_general(g, w_vmem[span, :], contract_last, preferred_element_type=f32)
            dx_send[:, spans[c], span] = value.astype(bf16).reshape(n, part_rows, size)

        tiles(part, body)
        for k in order:
            dx_copies[c, k] = send(
                dx_send.at[slot[k], spans[c]], dx_recv.at[slot[k], spans[c]], dx_sem, (c, k), k
            )
            dx_copies[c, k].start()

    dw_copies = []

    def weight(c):
        if c >= 2:
            dw_copies[c - 2].wait()
        span = slice(c * chunk, (c + 1) * chunk)

        def body(j, size):
            lines = pl.ds(pl.multiple_of(j * size, size), size)
            g = gathered[:, :, :, span].reshape(n * rows, chunk)
            dw_vmem[c % 2, lines, :] = jnp.dot(
                ni_t[lines, :], g, preferred_element_type=f32
            ).astype(bf16)

        tiles(part, body)
        copy = pltpu.make_async_copy(dw_vmem.at[c % 2], dw_hbm.at[:, span], dw_sem.at[c])
        copy.start()
        dw_copies.append(copy)

    def finish(c):
        inv = side_cols[0, spans[c], 0:1]
        total = jnp.zeros((part_rows, 1), f32)
        for k in [0] + order[::-1]:
            s = slot[k]
            if k:
                dx_copies[c, k].wait_recv()
            arrived = (dx_recv if k else dx_send)[s, spans[c], :].astype(f32)
            grad_hat = arrived * scales[s, spans[c], :]
            normed = x_ref[spans[c], columns(k)].astype(f32) * inv
            total = total + jnp.sum(grad_hat * normed, axis=-1, keepdims=True)
            scales[s, spans[c], :] = grad_hat
        mean = total / (n * part)
        for k in range(n):
            normed = x_ref[spans[c], columns(k)].astype(f32) * inv
            grad_ref[spans[c], columns(k)] = (
                inv * (scales[slot[k], spans[c], :] - normed * mean)
            ).astype(bf16)

    def outer_step():
        for copy in outer_copies:
            copy.wait_recv()
        terms = [outer_send[...].astype(f32)] + [
            outer_recv[k - 1].astype(f32) for k in range(1, replicas)
        ]
        while len(terms) > 1:
            terms = [terms[i] + terms[i + 1] for i in range(0, len(terms), 2)]
        average = terms[0] / replicas
        new_momentum = OUTER_MOMENTUM * momentum_ref[...] + average
        momentum_out[...] = new_momentum
        fragment_out[...] = params_ref[...] - OUTER_RATE * (
            average + OUTER_MOMENTUM * new_momentum
        )

    def table():
        frame_row = lax.broadcasted_iota(jnp.int32, (frame_count, rows), 0).astype(f32)
        summed = jnp.zeros((frame_count, part), f32)
        for s in range(n):
            normed = x_all[s].astype(f32) * side_cols[s, :, 0:1]
            picked = (sides[s, 1:2, :] == frame_row).astype(f32)
            summed = summed + jnp.dot(
                picked,
                dx_send[s].astype(f32) * normed,
                precision=EXACT,
                preferred_element_type=f32,
            )
        table_ref[...] = summed

    for t in range(CHUNKS + 4):
        if t < CHUNKS:
            project_tokens(t)
        if t == CHUNKS - 1:
            for s in range(n):
                ni_t[:, s * rows : (s + 1) * rows] = ni[s].astype(f32).T.astype(bf16)
        ready = 0 <= t - 3 < CHUNKS
        reducing = 0 <= t - 2 < CHUNKS
        if reducing:
            reduce_line(t - 2, 0)
        if ready:
            forward(t - 3, 0)
        if reducing:
            reduce_line(t - 2, 1)
        if 0 <= t - 1 < CHUNKS:
            reduce_pair(t - 1)
        if t == CHUNKS:
            outer_step()
        if ready:
            forward(t - 3, 1)
        if 0 <= t - 2 < CHUNKS:
            head_grads(t - 2)
        if ready:
            forward(t - 3, 2)
        if 0 <= t - 4 < CHUNKS:
            feature(t - 4)
    for c in range(CHUNKS):
        weight(c)
        if c < CHUNKS - 1:
            finish(c)
    table()
    finish(CHUNKS - 1)

    for copies in (x_copies, side_copies, gather_pair, dx_copies):
        for copy in copies.values():
            copy.wait_send()
    for (c, kz), copy in line_copies.items():
        if not passed_on or kz == 1:
            copy.wait_send()
    for (c, kz), copy in gather_line.items():
        if not passed_on or kz == 1:
            copy.wait_send()
    if passed_on:

        @pl.when(inner)
        def sent():
            for c in range(CHUNKS):
                for copy in (gather_line[c, 2], gather_line[c, 3], passes[c, 0], passes[c, 1]):
                    copy.wait_send()
                crossing[c, 2].wait_send()
                crossing[c, 3].wait_send()

        @pl.when(jnp.logical_not(inner))
        def sent_outer():
            for c in range(CHUNKS):
                line_copies[c, 2].wait_send()
                line_copies[c, 3].wait_send()

    for copy in pair_copies + outer_copies:
        copy.wait_send()
    for copy in dw_copies[-2:]:
        copy.wait()


def shards(
    clip_tokens,
    frame_ids,
    modulation,
    query_gain,
    query_weight,
    query_cotangent,
    pseudo_grad,
    outer_params,
    outer_momentum,
):
    n = lax.axis_size("fsdp")
    replicas = lax.axis_size("rep")
    rows, width = clip_tokens.shape
    part = width // n
    columns = query_weight.shape[2]
    chunk = columns // CHUNKS
    part_rows = rows // CHUNKS
    half = n // 2
    head = query_gain.shape[0]
    entries = outer_params.shape[0]
    fold = (entries // 128, 128)
    vmem = pl.BlockSpec(memory_space=pltpu.VMEM)
    hbm = pl.BlockSpec(memory_space=pl.ANY)
    dma = pltpu.SemaphoreType.DMA
    shape = jax.ShapeDtypeStruct
    outs = pl.pallas_call(
        functools.partial(kernel, n, replicas),
        out_shape=(
            shape((rows, width), bf16),
            shape((part, columns), bf16),
            shape((modulation.shape[0], part), f32),
            shape(fold, f32),
            shape(fold, f32),
        ),
        in_specs=[vmem] * 4 + [hbm] * 2 + [vmem] * 3,
        out_specs=(vmem, hbm, vmem, vmem, vmem),
        scratch_shapes=[
            pltpu.VMEM((part, columns), bf16),
            pltpu.VMEM((rows, columns), bf16),
            pltpu.VMEM((n, 8, rows), f32),
            pltpu.VMEM((n, rows, 8), f32),
            pltpu.VMEM((n, rows, part), bf16),
            pltpu.VMEM((n, rows, part), bf16),
            pltpu.VMEM((part, n * rows), bf16),
            pltpu.VMEM((CHUNKS, half, part_rows, columns), bf16),
            pltpu.VMEM((CHUNKS, half, part_rows, columns), bf16),
            pltpu.VMEM((CHUNKS, half, part_rows, columns), bf16),
            pltpu.VMEM((CHUNKS, half - 1, part_rows, columns), bf16),
            pltpu.VMEM((CHUNKS, 2, part_rows, columns) if half == 4 else (1, 1, 16, 128), bf16),
            pltpu.VMEM((2, part_rows, columns), f32),
            pltpu.VMEM((2, half, rows, columns), bf16),
            pltpu.VMEM((2, part, chunk), bf16),
            pltpu.VMEM((n, rows, part), f32),
            pltpu.VMEM((n, rows, part), bf16),
            pltpu.VMEM(fold, bf16),
            pltpu.VMEM((replicas - 1, *fold), bf16),
            dma((2,)),
            dma((CHUNKS,)),
            dma((2, replicas - 1)),
            dma((2, CHUNKS, n)),
            dma((2, n)),
            dma((2, CHUNKS)),
            dma((2, CHUNKS, half)),
            dma((2, CHUNKS, 2)),
            dma((2, CHUNKS, half)),
            dma((2, CHUNKS, half)),
            dma((CHUNKS, 2)),
            dma((2, CHUNKS, n)),
        ],
        compiler_params=pltpu.CompilerParams(
            collective_id=0, has_side_effects=True, vmem_limit_bytes=62 * 2**20
        ),
    )(
        clip_tokens,
        frame_ids.reshape(1, rows),
        modulation,
        query_gain.reshape(1, head),
        query_weight[0],
        query_cotangent,
        pseudo_grad.reshape(fold),
        outer_params.reshape(fold),
        outer_momentum.reshape(fold),
    )
    input_grad, weight_grad, table_grad, new_fragment, new_momentum = outs
    return (
        input_grad,
        weight_grad[None],
        table_grad[None],
        new_fragment.reshape(entries),
        new_momentum.reshape(entries),
    )


def solution(mesh):
    placed = (
        P(("rep", "fsdp"), None),
        P(("rep", "fsdp")),
        P(),
        P(),
        P("rep", "fsdp", None),
        P(("rep", "fsdp"), None),
        P("rep", "fsdp"),
        P("fsdp"),
        P("fsdp"),
    )
    return jax.shard_map(
        shards,
        mesh=mesh,
        in_specs=placed,
        out_specs=(
            P(("rep", "fsdp"), None),
            P("rep", "fsdp", None),
            P("rep", None, "fsdp"),
            P("fsdp"),
            P("fsdp"),
        ),
        check_vma=False,
    )
```
